32 devices in a mesh: row: 8 (over z, x), col: 4 (over y, core).
Axes of the slice: x: 2, y: 2, z: 4, core: 2. Of those that a mesh axis runs over, the one named last changes fastest.
Arguments:
- adjoints: bfloat16 [512, 16, 200], P(('row', 'col')), may hold values from -6 to 6
- jac_blocks: bfloat16 [8, 4, 128, 200, 200], P('row', 'col'), may hold values from -0.4375 to 0.4375
- jac_rows: int32 [8, 4, 128], P('row', 'col'), may hold values from 0 to 63, as said below
- jac_cols: int32 [8, 4, 128], P('row', 'col'), may hold values from 0 to 127, as said below
- tile_count: int32 [8, 4], P('row', 'col'), may hold values from 32 to 128, as said below
Outputs:
- transposed: bfloat16 [512, 16, 200], P('col')
The draws below stay inside these ranges and needn't reach their ends.
Inputs may be any that keep to these rules, and one draw needn't show every extreme that they name: `jac_rows`: row faces within a tile; both ends are named by some slot. `jac_cols`: column faces within a tile; both ends are named by some slot. `tile_count`: slots at or above the count are padding and are ignored; some tile has exactly 128 live slots.
All inputs are finite; a program needn't handle non-finite values.
Results may differ from the reference program's by a relative error of at most 0.001.
Values may be sent and summed in bfloat16 or wider, within the bound.
A program may use at most 64 MiB of HBM per device.

```python
import jax
import jax.numpy as jnp
from jax import lax

B = 200
K = 16
NB = 512
BROW = 64
BCOL = 128
CAP = 128
N_ROW = 8
N_COL = 4


def draw_jac_rows(key, part):
    row_index = jax.random.randint(jax.random.fold_in(key, 11), (N_ROW, N_COL, CAP), 0, BROW)
    row_index = row_index.at[0, 0, 0].set(BROW - 1).at[0, 0, 1].set(0)
    return row_index.astype(jnp.int32)


def draw_jac_cols(key, part):
    col_index = jax.random.randint(jax.random.fold_in(key, 23), (N_ROW, N_COL, CAP), 0, BCOL)
    col_index = col_index.at[0, 0, 0].set(0).at[0, 0, 1].set(BCOL - 1)
    return col_index.astype(jnp.int32)


def draw_tile_count(key, part):
    counts = jax.random.randint(jax.random.fold_in(key, 31), (N_ROW * N_COL,), CAP // 4, 3 * CAP // 4 + 1)
    chosen = jax.random.randint(jax.random.fold_in(key, 37), (), 0, N_ROW * N_COL)
    flattened = counts.at[chosen].set(CAP)
    return flattened.reshape((N_ROW, N_COL)).astype(jnp.int32)


def steps_of(own_key, shape, pieces, least, top_value):
    gain = 1.0
    for dim, shards_of in pieces:
        heights = jax.random.uniform(jax.random.fold_in(jax.random.fold_in(own_key, 6), dim), (shards_of,), jnp.float32, least / len(pieces), top_value / len(pieces))
        gain = gain * jnp.repeat(jnp.exp(heights), shape[dim] // shards_of).reshape((-1,) + (1,) * (len(shape) - 1 - dim))
    return gain


def normal_values(own_key, extent, deviation, limit, shards=(), kind=jnp.bfloat16):
    result = deviation * jax.random.normal(own_key, extent, jnp.float32)
    if shards:
        result = result * steps_of(own_key, extent, shards, -0.22, 0.18)
    return jnp.clip(result, -limit, limit).astype(kind)


def setup_inputs(seed: int = 0) -> dict:
    key_list = jax.random.split(jax.random.key(seed), 6)
    return {
        "adjoints": normal_values(key_list[0], (NB, K, B), 1.0, 6.0, ((0, 32),)),
        "jac_blocks": normal_values(key_list[1], (N_ROW, N_COL, CAP, B, B), B ** -0.5, 0.4375, ((0, 8), (1, 4))),
        "jac_rows": draw_jac_rows(jax.random.fold_in(key_list[5], 71), 0),
        "jac_cols": draw_jac_cols(jax.random.fold_in(key_list[5], 71), 0),
        "tile_count": draw_tile_count(jax.random.fold_in(key_list[5], 71), 0),
    }


def reference(adjoints, jac_blocks, jac_rows, jac_cols, tile_count):
    accumulated = jnp.zeros((NB, K, B), jnp.float32)

    def one_tile(running, tile_index):
        row_tile = tile_index // N_COL
        col_tile = tile_index % N_COL
        blocks = jac_blocks[row_tile, col_tile].astype(jnp.float32)
        face_rows = (row_tile * BROW + jac_rows[row_tile, col_tile]).astype(jnp.int32)
        picked = jnp.take(adjoints, face_rows, axis=0).astype(jnp.float32)
        products = jnp.einsum("skd,sde->ske", picked, blocks)
        live_slot = jnp.arange(CAP, dtype=jnp.int32) < tile_count[row_tile, col_tile]
        face_cols = jnp.where(live_slot, col_tile * BCOL + jac_cols[row_tile, col_tile], NB).astype(jnp.int32)
        running = running.at[face_cols].add(products, mode="drop")
        return running, None

    accumulated, _ = lax.scan(one_tile, accumulated, jnp.arange(N_ROW * N_COL, dtype=jnp.int32))
    return accumulated.astype(jnp.bfloat16)
```

```python
import functools

import jax
import jax.numpy as jnp
from jax import lax
from jax.experimental import pallas as pl
from jax.experimental.pallas import tpu as pltpu
from jax.sharding import PartitionSpec as P

MESH = pl.DeviceIdType.MESH
D_STEP = 8
E_CUTS = (0, 48, 96, 144)


def bit_count(n):
    return n.bit_length() - 1


def flip(index, bit):
    size = 2**bit
    return index + size - 2 * size * (index // size % 2)


class Flow:
    def __init__(self, index, base, group, e0, e1, order, n, me, refs):
        self.index, self.base, self.group, self.e0, self.e1 = index, base, group, e0, e1
        self.order, self.n, self.me, self.refs = order, n, me, refs
        self.off = 0
        self.length = n
        self.slot = 0
        self.stage = 0
        self.history = []
        self.sent = []
        self.pending = None

    def copy(self, src, dst, bit):
        refs = self.refs
        made = pltpu.make_async_remote_copy(
            src_ref=src,
            dst_ref=dst,
            send_sem=refs["send"].at[self.index, self.stage],
            recv_sem=refs["recv"].at[self.index, self.stage],
            device_id={"row": flip(self.me, bit)},
            device_id_type=MESH,
        )
        made.start()
        self.sent.append(made)
        self.pending = made

    def step(self):
        refs, rounds = self.refs, len(self.order)
        acc, land, whole = refs["acc"], refs["land"], refs["whole"]
        if self.stage > 2 * rounds:
            return
        e0, e1 = self.e0, self.e1
        e_end = -(-e1 // 16) * 16
        if self.stage:
            self.pending.wait_recv()
            if self.stage <= rounds:
                for i in range(self.length):
                    at = self.base + self.off + i
                    acc[at, e0:e1, :] = (
                        acc[at, e0:e1, :] + land[self.group, self.slot + i, e0:e1, :]
                    )
                self.slot += self.length
        if self.stage < rounds:
            bit = self.order[self.stage]
            half = self.length // 2
            mine = self.me // 2**bit % 2
            self.history.append((bit, self.off, self.length))
            there = self.base + self.off + (1 - mine) * half
            self.copy(
                acc.at[pl.ds(there, half), pl.ds(e0, e1 - e0), :],
                land.at[self.group, pl.ds(self.slot, half), pl.ds(e0, e1 - e0), :],
                bit,
            )
            self.off = self.off + mine * half
            self.length = half
        elif self.stage < 2 * rounds:
            if self.stage == rounds:
                value = acc[self.base + self.off, e0:e1, :]
                if e_end > e1:
                    tail = jnp.zeros((e_end - e1, value.shape[1]), jnp.float32)
                    value = jnp.concatenate([value, tail], axis=0)
                whole[self.base + self.off, e0:e_end, :] = value.astype(jnp.bfloat16)
            else:
                _, self.off, self.length = self.history.pop()
            bit = self.history[-1][0]
            part = whole.at[
                pl.ds(self.base + self.off, self.length), pl.ds(e0, e_end - e0), :
            ]
            self.copy(part, part, bit)
        self.stage += 1


def kernel(
    n_row, n_col,
    adj_ref, blocks_ref, rows_ref, cols_ref, count_ref, out_ref,
    adj_all, adj_wide, picked, block_buf, factor, acc, land, whole,
    block_sem, adj_send, adj_recv, send, recv,
):
    row, col = lax.axis_index("row"), lax.axis_index("col")
    row_bits, col_bits = bit_count(n_row), bit_count(n_col)
    faces, functionals, dofs = adj_ref.shape
    slots = rows_ref.shape[1]
    columns = out_ref.shape[2]
    row_faces = faces * n_col

    fetch = pltpu.make_async_copy(blocks_ref, block_buf, block_sem)
    fetch.start()

    barrier = pltpu.get_barrier_semaphore()
    for bit in range(row_bits):
        pl.semaphore_signal(barrier, inc=1, device_id={"row": flip(row, bit)}, device_id_type=MESH)
    for bit in range(col_bits):
        pl.semaphore_signal(barrier, inc=1, device_id={"col": flip(col, bit)}, device_id_type=MESH)
    pl.semaphore_wait(barrier, row_bits + col_bits)

    adj_all[pl.ds(col * faces, faces)] = adj_ref[...]
    sends = []
    for number, bit in enumerate(reversed(range(col_bits))):
        copies = []
        stride = 2 ** (bit + 1)
        for i in range(2**number):
            shard = col % stride + i * stride
            part = adj_all.at[pl.ds(shard * faces, faces)]
            made = pltpu.make_async_remote_copy(
                src_ref=part,
                dst_ref=part,
                send_sem=adj_send.at[2**number - 1 + i],
                recv_sem=adj_recv.at[2**number - 1 + i],
                device_id={"col": flip(col, bit)},
                device_id_type=MESH,
            )
            made.start()
            copies.append(made)
        for made in copies:
            made.wait_recv()
        sends += copies

    wide = adj_all[...].astype(jnp.float32).reshape(row_faces * functionals, dofs)
    pieces = [(at, min(dofs - at, 128)) for at in range(0, dofs, 128)]
    for i, (at, size) in enumerate(pieces):
        adj_wide[i, :, :size] = wide[:, at : at + size]
    chosen = (
        lax.broadcasted_iota(jnp.int32, (row_faces, slots), 0) == rows_ref[...]
    ).astype(jnp.float32).astype(jnp.bfloat16)
    for k in range(functionals):
        for i, (at, size) in enumerate(pieces):
            rows_k = adj_wide.at[i][pl.ds(k, row_faces, stride=functionals), :]
            found = lax.dot_general(
                rows_k[:, :size].astype(jnp.bfloat16),
                chosen,
                (((0,), (0,)), ((), ())),
                preferred_element_type=jnp.float32,
            )
            picked[pl.ds(k * dofs + at, size), :] = found
    live = lax.broadcasted_iota(jnp.int32, (columns, slots), 1) < count_ref[0, 0]
    named = lax.broadcasted_iota(jnp.int32, (columns, slots), 0) == cols_ref[...]
    selector = (live & named).astype(jnp.float32).astype(jnp.bfloat16)
    fetch.wait()

    def pair(k0):
        acc[k0] = jnp.zeros((dofs, columns), jnp.float32)
        acc[k0 + 1] = jnp.zeros((dofs, columns), jnp.float32)

        def some(step, _):
            d0 = pl.multiple_of(step * D_STEP, D_STEP)
            left = jnp.concatenate([block_buf[d0 + i] for i in range(D_STEP)], axis=1)
            for side in range(2):
                values = picked[pl.ds((k0 + side) * dofs + d0, D_STEP), :]
                for i in range(D_STEP):
                    wide = jnp.broadcast_to(values[i : i + 1, :], (16, slots)).astype(jnp.bfloat16)
                    tiled = jnp.concatenate([wide] * (columns // 16), axis=0)
                    factor[pl.ds(side * columns, columns), pl.ds(i * slots, slots)] = tiled * selector
            product = lax.dot_general(
                left, factor[...], (((1,), (1,)), ((), ())), preferred_element_type=jnp.float32
            )
            acc[k0] += product[:, :columns]
            acc[k0 + 1] += product[:, columns:]
            return 0

        lax.fori_loop(0, dofs // D_STEP, some, 0)

    refs = {"acc": acc, "land": land, "whole": whole, "send": send, "recv": recv}
    groups = functionals // n_row
    flows = []
    for group in range(groups):
        for at in range(0, n_row, 2):
            pair(group * n_row + at)
            for flow in flows:
                flow.step()
        fresh = []
        for i, e0 in enumerate(E_CUTS):
            e1 = E_CUTS[i + 1] if i + 1 < len(E_CUTS) else dofs
            order = list(range(row_bits))
            if i == 0:
                order[0], order[1] = order[1], order[0]
            fresh.append(
                Flow(len(flows) + i, group * n_row, group, e0, e1, order, n_row, row, refs)
            )
        for flow in fresh:
            flow.step()
        flows += fresh
    for _ in range(2 * row_bits):
        for flow in flows:
            flow.step()
    out_ref[...] = whole[:, :dofs, :]
    for flow in flows:
        for made in flow.sent:
            made.wait_send()
    for made in sends:
        made.wait_send()


def on_device(n_row, n_col, adjoints, jac_blocks, jac_rows, jac_cols, tile_count):
    faces, functionals, dofs = adjoints.shape
    slots = jac_rows.shape[-1]
    columns = faces * n_row
    row_faces = faces * n_col
    groups = functionals // n_row
    n_flows = groups * len(E_CUTS)
    rounds = bit_count(n_row)
    padded = -(-dofs // 16) * 16
    blocks = jnp.transpose(jac_blocks[0, 0], (1, 2, 0))
    vmem = pl.BlockSpec(memory_space=pltpu.VMEM)
    out = pl.pallas_call(
        functools.partial(kernel, n_row, n_col),
        out_shape=jax.ShapeDtypeStruct((functionals, dofs, columns), jnp.bfloat16),
        in_specs=[
            vmem,
            pl.BlockSpec(memory_space=pl.ANY),
            vmem,
            vmem,
            pl.BlockSpec(memory_space=pltpu.SMEM),
        ],
        out_specs=vmem,
        scratch_shapes=[
            pltpu.VMEM((row_faces, functionals, dofs), jnp.bfloat16),
            pltpu.VMEM((-(-dofs // 128), row_faces * functionals, 128), jnp.float32),
            pltpu.VMEM((functionals * dofs, slots), jnp.float32),
            pltpu.VMEM((dofs, dofs, slots), jnp.bfloat16),
            pltpu.VMEM((2 * columns, D_STEP * slots), jnp.bfloat16),
            pltpu.VMEM((functionals, dofs, columns), jnp.float32),
            pltpu.VMEM((groups, n_row - 1, dofs, columns), jnp.float32),
            pltpu.VMEM((functionals, padded, columns), jnp.bfloat16),
            pltpu.SemaphoreType.DMA,
            pltpu.SemaphoreType.DMA((n_col - 1,)),
            pltpu.SemaphoreType.DMA((n_col - 1,)),
            pltpu.SemaphoreType.DMA((n_flows, 2 * rounds)),
            pltpu.SemaphoreType.DMA((n_flows, 2 * rounds)),
        ],
        compiler_params=pltpu.CompilerParams(
            collective_id=0, has_side_effects=True, vmem_limit_bytes=48 * 2**20
        ),
    )(adjoints, blocks, jac_rows[0], jac_cols[0], tile_count)
    return jnp.transpose(out, (2, 0, 1))


def solution(mesh):
    placed = (
        P(("row", "col"), None, None),
        P("row", "col", None, None, None),
        P("row", "col", None),
        P("row", "col", None),
        P("row", "col"),
    )
    return jax.shard_map(
        functools.partial(on_device, mesh.shape["row"], mesh.shape["col"]),
        mesh=mesh,
        in_specs=placed,
        out_specs=P("col", None, None),
        check_vma=False,
    )
```

```python
import functools

import jax
import jax.numpy as jnp
from jax import lax
from jax.experimental import pallas as pl
from jax.experimental.pallas import tpu as pltpu
from jax.sharding import PartitionSpec as P

MESH = pl.DeviceIdType.MESH
D_STEP = 40
E_CUTS = (0, 48)
TOGETHER = 4


def bit_count(n):
    return n.bit_length() - 1


def flip(index, bit):
    size = 2**bit
    return index + size - 2 * size * (index // size % 2)


class Flow:
    def __init__(self, index, base, group, e0, e1, order, n, me, refs):
        self.index, self.base, self.group, self.e0, self.e1 = index, base, group, e0, e1
        self.order, self.n, self.me, self.refs = order, n, me, refs
        self.off = 0
        self.length = n
        self.slot = 0
        self.stage = 0
        self.history = []
        self.sent = []
        self.pending = None

    def copy(self, src, dst, bit):
        refs = self.refs
        made = pltpu.make_async_remote_copy(
            src_ref=src,
            dst_ref=dst,
            send_sem=refs["send"].at[self.index, self.stage],
            recv_sem=refs["recv"].at[self.index, self.stage],
            device_id={"row": flip(self.me, bit)},
            device_id_type=MESH,
        )
        made.start()
        self.sent.append(made)
        self.pending = made

    def step(self):
        refs, rounds = self.refs, len(self.order)
        acc, land, whole = refs["acc"], refs["land"], refs["whole"]
        if self.stage > 2 * rounds:
            return
        e0, e1 = self.e0, self.e1
        if self.stage:
            self.pending.wait_recv()
            if self.stage <= rounds:
                for i in range(self.length):
                    at = self.base + self.off + i
                    acc[at, e0:e1, :] = (
                        acc[at, e0:e1, :] + land[self.group, self.slot + i, e0:e1, :]
                    )
                self.slot += self.length
        if self.stage < rounds:
            bit = self.order[self.stage]
            half = self.length // 2
            mine = self.me // 2**bit % 2
            self.history.append((bit, self.off, self.length))
            there = self.base + self.off + (1 - mine) * half
            self.copy(
                acc.at[pl.ds(there, half), pl.ds(e0, e1 - e0), :],
                land.at[self.group, pl.ds(self.slot, half), pl.ds(e0, e1 - e0), :],
                bit,
            )
            self.off = self.off + mine * half
            self.length = half
        elif self.stage < 2 * rounds:
            if self.stage == rounds:
                value = acc[self.base + self.off, e0:e1, :]
                whole[self.base + self.off, e0:e1, :] = value.astype(jnp.bfloat16)
            else:
                _, self.off, self.length = self.history.pop()
            bit = self.history[-1][0]
            part = whole.at[
                pl.ds(self.base + self.off, self.length), pl.ds(e0, e1 - e0), :
            ]
            self.copy(part, part, bit)
        self.stage += 1


def kernel(
    n_row, n_col,
    adj_ref, blocks_ref, rows_ref, cols_ref, count_ref, out_ref,
    adj_all, adj_wide, picked, block_buf, factor, acc, land, whole,
    block_sem, adj_send, adj_recv, send, recv,
):
    row, col = lax.axis_index("row"), lax.axis_index("col")
    row_bits, col_bits = bit_count(n_row), bit_count(n_col)
    faces, functionals, dofs = adj_ref.shape
    slots = rows_ref.shape[1]
    columns = out_ref.shape[2]
    row_faces = faces * n_col

    fetch = pltpu.make_async_copy(blocks_ref, block_buf, block_sem)
    fetch.start()

    barrier = pltpu.get_barrier_semaphore()
    for bit in range(row_bits):
        pl.semaphore_signal(barrier, inc=1, device_id={"row": flip(row, bit)}, device_id_type=MESH)
    for bit in range(col_bits):
        pl.semaphore_signal(barrier, inc=1, device_id={"col": flip(col, bit)}, device_id_type=MESH)
    pl.semaphore_wait(barrier, row_bits + col_bits)

    adj_all[pl.ds(col * faces, faces)] = adj_ref[...]
    sends = []
    for number, bit in enumerate(reversed(range(col_bits))):
        copies = []
        stride = 2 ** (bit + 1)
        for i in range(2**number):
            shard = col % stride + i * stride
            part = adj_all.at[pl.ds(shard * faces, faces)]
            made = pltpu.make_async_remote_copy(
                src_ref=part,
                dst_ref=part,
                send_sem=adj_send.at[2**number - 1 + i],
                recv_sem=adj_recv.at[2**number - 1 + i],
                device_id={"col": flip(col, bit)},
                device_id_type=MESH,
            )
            made.start()
            copies.append(made)
        for made in copies:
            made.wait_recv()
        sends += copies

    wide = adj_all[...].astype(jnp.float32).reshape(row_faces * functionals, dofs)
    pieces = [(at, min(dofs - at, 128)) for at in range(0, dofs, 128)]
    for i, (at, size) in enumerate(pieces):
        adj_wide[i, :, :size] = wide[:, at : at + size]
    chosen = (
        lax.broadcasted_iota(jnp.int32, (row_faces, slots), 0) == rows_ref[...]
    ).astype(jnp.float32).astype(jnp.bfloat16)
    for k in range(functionals):
        for i, (at, size) in enumerate(pieces):
            rows_k = adj_wide.at[i][pl.ds(k, row_faces, stride=functionals), :]
            found = lax.dot_general(
                rows_k[:, :size].astype(jnp.bfloat16),
                chosen,
                (((0,), (0,)), ((), ())),
                preferred_element_type=jnp.float32,
            )
            picked[pl.ds(k * dofs + at, size), :] = found
    live = lax.broadcasted_iota(jnp.int32, (columns, slots), 1) < count_ref[0, 0]
    named = lax.broadcasted_iota(jnp.int32, (columns, slots), 0) == cols_ref[...]
    selector = (live & named).astype(jnp.float32).astype(jnp.bfloat16)
    fetch.wait()

    parts = n_row // TOGETHER
    rows = acc.shape[1]
    cuts = [(p, p * rows, min(rows, dofs - p * rows)) for p in range(parts)]

    def pair(k0):
        acc[pl.ds(k0 * parts, 2 * parts)] = jnp.zeros((2 * parts, rows, columns), jnp.float32)

        def some(step, _):
            d0 = pl.multiple_of(step * D_STEP, D_STEP)
            left = jnp.concatenate([block_buf[d0 + i] for i in range(D_STEP)], axis=1)
            for side in range(2):
                values = picked[pl.ds((k0 + side) * dofs + d0, D_STEP), :]
                for i in range(D_STEP):
                    wide = jnp.broadcast_to(values[i : i + 1, :], (16, slots)).astype(jnp.bfloat16)
                    tiled = jnp.concatenate([wide] * (columns // 16), axis=0)
                    factor[pl.ds(side * columns, columns), pl.ds(i * slots, slots)] = tiled * selector
            product = lax.dot_general(
                left, factor[...], (((1,), (1,)), ((), ())), preferred_element_type=jnp.float32
            )
            for side in range(2):
                for p, at, size in cuts:
                    acc[(k0 + side) * parts + p, :size, :] += product[
                        at : at + size, side * columns : (side + 1) * columns
                    ]
            return 0

        lax.fori_loop(0, dofs // D_STEP, some, 0)

    refs = {"acc": acc, "land": land, "whole": whole, "send": send, "recv": recv}
    flows = []
    for group in range(functionals // TOGETHER):
        for at in range(0, TOGETHER, 2):
            pair(group * TOGETHER + at)
            for flow in flows:
                flow.step()
        fresh = []
        for i, e0 in enumerate(E_CUTS):
            e1 = E_CUTS[i + 1] if i + 1 < len(E_CUTS) else rows
            order = list(range(row_bits))
            if i == 0:
                order[0], order[1] = order[1], order[0]
            fresh.append(
                Flow(len(flows) + i, group * n_row, group, e0, e1, order, n_row, row, refs)
            )
        for flow in fresh:
            flow.step()
        flows += fresh
    for _ in range(2 * row_bits):
        for flow in flows:
            flow.step()
    for k in range(functionals):
        for p, at, size in cuts:
            out_ref[k, pl.ds(at, size), :] = whole[k * parts + p, :size, :]
    for flow in flows:
        for made in flow.sent:
            made.wait_send()
    for made in sends:
        made.wait_send()


def on_device(n_row, n_col, adjoints, jac_blocks, jac_rows, jac_cols, tile_count):
    faces, functionals, dofs = adjoints.shape
    slots = jac_rows.shape[-1]
    columns = faces * n_row
    row_faces = faces * n_col
    groups = functionals // TOGETHER
    parts = n_row // TOGETHER
    n_flows = groups * len(E_CUTS)
    rounds = bit_count(n_row)
    rows = -(-dofs // (16 * parts)) * 16
    blocks = jnp.transpose(jac_blocks[0, 0], (1, 2, 0))
    vmem = pl.BlockSpec(memory_space=pltpu.VMEM)
    out = pl.pallas_call(
        functools.partial(kernel, n_row, n_col),
        out_shape=jax.ShapeDtypeStruct((functionals, dofs, columns), jnp.bfloat16),
        in_specs=[
            vmem,
            pl.BlockSpec(memory_space=pl.ANY),
            vmem,
            vmem,
            pl.BlockSpec(memory_space=pltpu.SMEM),
        ],
        out_specs=vmem,
        scratch_shapes=[
            pltpu.VMEM((row_faces, functionals, dofs), jnp.bfloat16),
            pltpu.VMEM((-(-dofs // 128), row_faces * functionals, 128), jnp.float32),
            pltpu.VMEM((functionals * dofs, slots), jnp.float32),
            pltpu.VMEM((dofs, dofs, slots), jnp.bfloat16),
            pltpu.VMEM((2 * columns, D_STEP * slots), jnp.bfloat16),
            pltpu.VMEM((functionals * parts, rows, columns), jnp.float32),
            pltpu.VMEM((groups, n_row - 1, rows, columns), jnp.float32),
            pltpu.VMEM((functionals * parts, rows, columns), jnp.bfloat16),
            pltpu.SemaphoreType.DMA,
            pltpu.SemaphoreType.DMA((n_col - 1,)),
            pltpu.SemaphoreType.DMA((n_col - 1,)),
            pltpu.SemaphoreType.DMA((n_flows, 2 * rounds)),
            pltpu.SemaphoreType.DMA((n_flows, 2 * rounds)),
        ],
        compiler_params=pltpu.CompilerParams(
            collective_id=0, has_side_effects=True, vmem_limit_bytes=48 * 2**20
        ),
    )(adjoints, blocks, jac_rows[0], jac_cols[0], tile_count)
    return jnp.transpose(out, (2, 0, 1))


def solution(mesh):
    placed = (
        P(("row", "col"), None, None),
        P("row", "col", None, None, None),
        P("row", "col", None),
        P("row", "col", None),
        P("row", "col"),
    )
    return jax.shard_map(
        functools.partial(on_device, mesh.shape["row"], mesh.shape["col"]),
        mesh=mesh,
        in_specs=placed,
        out_specs=P("col", None, None),
        check_vma=False,
    )
```

```python
import functools

import jax
import jax.numpy as jnp
from jax import lax
from jax.experimental import pallas as pl
from jax.experimental.pallas import tpu as pltpu
from jax.sharding import PartitionSpec as P

MESH = pl.DeviceIdType.MESH
D_STEP = 40
E_CUTS = (0, 48)
TOGETHER = 4


def bit_count(n):
    return n.bit_length() - 1


def flip(index, bit):
    size = 2**bit
    return index + size - 2 * size * (index // size % 2)


class Flow:
    def __init__(self, index, base, group, e0, e1, order, n, me, refs):
        self.index, self.base, self.group, self.e0, self.e1 = index, base, group, e0, e1
        self.order, self.n, self.me, self.refs = order, n, me, refs
        self.off = 0
        self.length = n
        self.slot = 0
        self.stage = 0
        self.history = []
        self.sent = []
        self.pending = None

    def copy(self, src, dst, bit):
        refs = self.refs
        made = pltpu.make_async_remote_copy(
            src_ref=src,
            dst_ref=dst,
            send_sem=refs["send"].at[self.index, self.stage],
            recv_sem=refs["recv"].at[self.index, self.stage],
            device_id={"row": flip(self.me, bit)},
            device_id_type=MESH,
        )
        made.start()
        self.sent.append(made)
        self.pending = made

    def step(self):
        refs, rounds = self.refs, len(self.order)
        acc, land, whole = refs["acc"], refs["land"], refs["whole"]
        if self.stage > 2 * rounds:
            return
        e0, e1 = self.e0, self.e1
        if self.stage:
            self.pending.wait_recv()
            if self.stage <= rounds:
                for i in range(self.length):
                    at = self.base + self.off + i
                    acc[at, e0:e1, :] = (
                        acc[at, e0:e1, :] + land[self.group, self.slot + i, e0:e1, :]
                    )
                self.slot += self.length
        if self.stage < rounds:
            bit = self.order[self.stage]
            half = self.length // 2
            mine = self.me // 2**bit % 2
            self.history.append((bit, self.off, self.length))
            there = self.base + self.off + (1 - mine) * half
            self.copy(
                acc.at[pl.ds(there, half), pl.ds(e0, e1 - e0), :],
                land.at[self.group, pl.ds(self.slot, half), pl.ds(e0, e1 - e0), :],
                bit,
            )
            self.off = self.off + mine * half
            self.length = half
        elif self.stage < 2 * rounds:
            if self.stage == rounds:
                value = acc[self.base + self.off, e0:e1, :]
                whole[self.base + self.off, e0:e1, :] = value.astype(jnp.bfloat16)
            else:
                _, self.off, self.length = self.history.pop()
            bit = self.history[-1][0]
            part = whole.at[
                pl.ds(self.base + self.off, self.length), pl.ds(e0, e1 - e0), :
            ]
            self.copy(part, part, bit)
        self.stage += 1


def kernel(
    n_row, n_col,
    adj_ref, blocks_ref, rows_ref, cols_ref, count_ref, out_ref,
    adj_all, adj_wide, picked, block_buf, factor, acc, land, whole,
    block_sem, adj_send, adj_recv, send, recv,
):
    row, col = lax.axis_index("row"), lax.axis_index("col")
    row_bits, col_bits = bit_count(n_row), bit_count(n_col)
    faces, functionals, dofs = adj_ref.shape
    slots = rows_ref.shape[1]
    columns = out_ref.shape[2]
    row_faces = faces * n_col

    fetch = pltpu.make_async_copy(blocks_ref, block_buf, block_sem)
    fetch.start()

    barrier = pltpu.get_barrier_semaphore()
    for bit in range(row_bits):
        pl.semaphore_signal(barrier, inc=1, device_id={"row": flip(row, bit)}, device_id_type=MESH)
    for bit in range(col_bits):
        pl.semaphore_signal(barrier, inc=1, device_id={"col": flip(col, bit)}, device_id_type=MESH)
    pl.semaphore_wait(barrier, row_bits + col_bits)

    adj_all[pl.ds(col * faces, faces)] = adj_ref[...]
    sends = []
    for number, bit in enumerate(reversed(range(col_bits))):
        copies = []
        stride = 2 ** (bit + 1)
        for i in range(2**number):
            shard = col % stride + i * stride
            part = adj_all.at[pl.ds(shard * faces, faces)]
            made = pltpu.make_async_remote_copy(
                src_ref=part,
                dst_ref=part,
                send_sem=adj_send.at[2**number - 1 + i],
                recv_sem=adj_recv.at[2**number - 1 + i],
                device_id={"col": flip(col, bit)},
                device_id_type=MESH,
            )
            made.start()
            copies.append(made)
        for made in copies:
            made.wait_recv()
        sends += copies

    wide = adj_all[...].astype(jnp.float32).reshape(row_faces * functionals, dofs)
    pieces = [(at, min(dofs - at, 128)) for at in range(0, dofs, 128)]
    for i, (at, size) in enumerate(pieces):
        adj_wide[i, :, :size] = wide[:, at : at + size]
    chosen = (
        lax.broadcasted_iota(jnp.int32, (row_faces, slots), 0) == rows_ref[...]
    ).astype(jnp.float32).astype(jnp.bfloat16)
    for k in range(functionals):
        for i, (at, size) in enumerate(pieces):
            rows_k = adj_wide.at[i][pl.ds(k, row_faces, stride=functionals), :]
            found = lax.dot_general(
                rows_k[:, :size].astype(jnp.bfloat16),
                chosen,
                (((0,), (0,)), ((), ())),
                preferred_element_type=jnp.float32,
            )
            picked[pl.ds(k * dofs + at, size), :] = found
    live = lax.broadcasted_iota(jnp.int32, (columns, slots), 1) < count_ref[0, 0]
    named = lax.broadcasted_iota(jnp.int32, (columns, slots), 0) == cols_ref[...]
    selector = (live & named).astype(jnp.float32).astype(jnp.bfloat16)
    fetch.wait()

    parts = n_row // TOGETHER
    rows = acc.shape[1]
    cuts = [(p, p * rows, min(rows, dofs - p * rows)) for p in range(parts)]

    def pair(k0):
        acc[pl.ds(k0 * parts, 2 * parts)] = jnp.zeros((2 * parts, rows, columns), jnp.float32)

        def some(step, _):
            d0 = pl.multiple_of(step * D_STEP, D_STEP)
            left = jnp.concatenate([block_buf[d0 + i] for i in range(D_STEP)], axis=1)
            for side in range(2):
                values = picked[pl.ds((k0 + side) * dofs + d0, D_STEP), :]
                for i in range(D_STEP):
                    wide = jnp.broadcast_to(values[i : i + 1, :], (16, slots)).astype(jnp.bfloat16)
                    tiled = jnp.concatenate([wide] * (columns // 16), axis=0)
                    factor[pl.ds(side * columns, columns), pl.ds(i * slots, slots)] = tiled * selector
            product = lax.dot_general(
                left, factor[...], (((1,), (1,)), ((), ())), preferred_element_type=jnp.float32
            )
            for side in range(2):
                for p, at, size in cuts:
                    acc[(k0 + side) * parts + p, :size, :] += product[
                        at : at + size, side * columns : (side + 1) * columns
                    ]
            return 0

        lax.fori_loop(0, dofs // D_STEP, some, 0)

    refs = {"acc": acc, "land": land, "whole": whole, "send": send, "recv": recv}
    flows = []
    for group in range(functionals // TOGETHER):
        for at in range(0, TOGETHER, 2):
            pair(group * TOGETHER + at)
            if at + 2 < TOGETHER:
                for flow in flows:
                    flow.step()
        fresh = []
        for i, e0 in enumerate(E_CUTS):
            e1 = E_CUTS[i + 1] if i + 1 < len(E_CUTS) else rows
            order = list(range(row_bits))
            if i == 0:
                order[0], order[1] = order[1], order[0]
            fresh.append(
                Flow(len(flows) + i, group * n_row, group, e0, e1, order, n_row, row, refs)
            )
        for flow in fresh:
            flow.step()
        for flow in flows:
            flow.step()
        flows += fresh
    for _ in range(2 * row_bits):
        for flow in flows:
            flow.step()
    for k in range(functionals):
        for p, at, size in cuts:
            out_ref[k, pl.ds(at, size), :] = whole[k * parts + p, :size, :]
    for flow in flows:
        for made in flow.sent:
            made.wait_send()
    for made in sends:
        made.wait_send()


def on_device(n_row, n_col, adjoints, jac_blocks, jac_rows, jac_cols, tile_count):
    faces, functionals, dofs = adjoints.shape
    slots = jac_rows.shape[-1]
    columns = faces * n_row
    row_faces = faces * n_col
    groups = functionals // TOGETHER
    parts = n_row // TOGETHER
    n_flows = groups * len(E_CUTS)
    rounds = bit_count(n_row)
    rows = -(-dofs // (16 * parts)) * 16
    blocks = jnp.transpose(jac_blocks[0, 0], (1, 2, 0))
    vmem = pl.BlockSpec(memory_space=pltpu.VMEM)
    out = pl.pallas_call(
        functools.partial(kernel, n_row, n_col),
        out_shape=jax.ShapeDtypeStruct((functionals, dofs, columns), jnp.bfloat16),
        in_specs=[
            vmem,
            pl.BlockSpec(memory_space=pl.ANY),
            vmem,
            vmem,
            pl.BlockSpec(memory_space=pltpu.SMEM),
        ],
        out_specs=vmem,
        scratch_shapes=[
            pltpu.VMEM((row_faces, functionals, dofs), jnp.bfloat16),
            pltpu.VMEM((-(-dofs // 128), row_faces * functionals, 128), jnp.float32),
            pltpu.VMEM((functionals * dofs, slots), jnp.float32),
            pltpu.VMEM((dofs, dofs, slots), jnp.bfloat16),
            pltpu.VMEM((2 * columns, D_STEP * slots), jnp.bfloat16),
            pltpu.VMEM((functionals * parts, rows, columns), jnp.float32),
            pltpu.VMEM((groups, n_row - 1, rows, columns), jnp.float32),
            pltpu.VMEM((functionals * parts, rows, columns), jnp.bfloat16),
            pltpu.SemaphoreType.DMA,
            pltpu.SemaphoreType.DMA((n_col - 1,)),
            pltpu.SemaphoreType.DMA((n_col - 1,)),
            pltpu.SemaphoreType.DMA((n_flows, 2 * rounds)),
            pltpu.SemaphoreType.DMA((n_flows, 2 * rounds)),
        ],
        compiler_params=pltpu.CompilerParams(
            collective_id=0, has_side_effects=True, vmem_limit_bytes=48 * 2**20
        ),
    )(adjoints, blocks, jac_rows[0], jac_cols[0], tile_count)
    return jnp.transpose(out, (2, 0, 1))


def solution(mesh):
    placed = (
        P(("row", "col"), None, None),
        P("row", "col", None, None, None),
        P("row", "col", None),
        P("row", "col", None),
        P("row", "col"),
    )
    return jax.shard_map(
        functools.partial(on_device, mesh.shape["row"], mesh.shape["col"]),
        mesh=mesh,
        in_specs=placed,
        out_specs=P("col", None, None),
        check_vma=False,
    )
```
